32 devices in a mesh: mp: 2 (over core), heads: 8 (over z, y), tok: 2 (over x).
Axes of the slice: x: 2, y: 2, z: 4, core: 2. Of those that a mesh axis runs over, the one named last changes fastest.
Arguments:
- context: bfloat16 [2, 512, 8192], P('mp', None, 'heads'), may hold values from -6 to 6
- out_weight: bfloat16 [2, 8192, 8192], P('mp', 'heads', 'tok'), may hold values from -0.0625 to 0.0625
- skip_states: bfloat16 [2, 512, 8192], P(None, None, 'tok'), may hold values from -6 to 6
- gram_old: float32 [8192, 8192], P('tok', ('mp', 'heads')), may hold values from -1 to 3
- cross_old: float32 [8192, 8192], P('tok', ('mp', 'heads')), may hold values from -30 to 30
- map_old: float32 [8192, 8192], P('tok', ('mp', 'heads')), may hold values from -0.3 to 0.3
Outputs:
- gram_new: float32 [8192, 8192], P('tok', ('mp', 'heads'))
- cross_new: float32 [8192, 8192], P('tok', ('mp', 'heads'))
- map_new: float32 [8192, 8192], P('tok', ('mp', 'heads'))
- residual_new: float32 [8192, 8192], P('tok', ('mp', 'heads'))
The draws below stay inside these ranges and needn't reach their ends.
All inputs are finite; a program needn't handle non-finite values.
Results may differ from the reference program's by a relative error of at most 0.03.
Values may be sent and summed in bfloat16 or wider, within the bound.
A program may use at most 256 MiB of HBM per device.

```python
import math
import jax
import jax.numpy as jnp
from jax import lax

D = 8192
NH = 64
HD = 128
TOKENS = 512
N_HEADS = 8


def draw_gram_old(key, part):
    first_key, second_key = jax.random.split(jax.random.fold_in(key, 11))
    highest = 2.0
    uniform_base = jax.random.uniform(first_key, (D, D), jnp.float32, -1.0, 1.0)
    off_part = (uniform_base + uniform_base.T) * (0.35 / math.sqrt(D))
    spread = jax.random.uniform(second_key, (D,), jnp.float32, 0.0, 1.0)
    diagonal = jnp.exp(spread * math.log(highest))
    row_ids = lax_iota_rows()
    on_diagonal = row_ids[:, None] == row_ids[None, :]
    return jnp.where(on_diagonal, diagonal[:, None] * jnp.ones((1, D), jnp.float32), off_part)


def lax_iota_rows():
    return jnp.arange(D, dtype=jnp.int32)


def draw_cross_old(key, part):
    keys = jax.random.split(jax.random.fold_in(key, 23), 3)
    row_scale = jnp.exp(jax.random.uniform(keys[0], (D,), jnp.float32, 0.0, 1.0) * math.log(10.0))
    col_scale = jnp.exp(jax.random.uniform(keys[1], (D,), jnp.float32, 0.0, 1.0) * math.log(10.0))
    ramp = jnp.exp(0.5 * math.log(3.0) * jnp.arange(D, dtype=jnp.float32) / D)
    values = jnp.clip(jax.random.normal(keys[2], (D, D), jnp.float32), -4.0, 4.0)
    return 0.02 * values * (row_scale * ramp)[:, None] * (col_scale * ramp)[None, :]


def shard_levels(rng, dims, pieces, low, top_value):
    def one(dim, parts):
        draws = jax.random.uniform(jax.random.fold_in(jax.random.fold_in(rng, 6), dim), (parts,), jnp.float32, low / len(pieces), top_value / len(pieces))
        return jnp.repeat(jnp.exp(draws), dims[dim] // parts).reshape((-1,) + (1,) * (len(dims) - dim - 1))

    level = one(*pieces[0])
    for cut in pieces[1:]:
        level = level * one(*cut)
    return level


def bell_draw(rng, extent, width, limit, shards=(), kind=jnp.bfloat16):
    result = width * jax.random.normal(rng, extent, jnp.float32)
    if shards:
        result = result * shard_levels(rng, extent, shards, -0.22, 0.18)
    return jnp.clip(result, -limit, limit).astype(kind)


def setup_inputs(seed: int = 0) -> dict:
    splits = jax.random.split(jax.random.key(seed), 7)
    context = bell_draw(splits[0], (2, TOKENS, NH * HD), 1.0, 6.0, ((0, 2), (2, 8)))
    out_weight = bell_draw(splits[1], (2, NH * HD, D), (NH * HD) ** -0.5, 0.0625, ((0, 2), (1, 8), (2, 2)))
    skip_states = bell_draw(splits[2], (2, TOKENS, D), 1.0, 6.0, ((2, 2),))
    gram_old = draw_gram_old(jax.random.fold_in(splits[6], 71), 0)
    cross_old = draw_cross_old(jax.random.fold_in(splits[6], 71), 0)
    map_old = bell_draw(splits[5], (D, D), 0.05, 0.3, ((0, 2), (1, 16)), jnp.float32)
    return dict(context=context, out_weight=out_weight, skip_states=skip_states, gram_old=gram_old, cross_old=cross_old, map_old=map_old)


decay_keep = 0.75
ridge_weight = 0.1


def model_states(context_one, weight_one, skip_one):
    group_width = context_one.shape[1] // N_HEADS
    running = jnp.zeros((context_one.shape[0], weight_one.shape[1]), jnp.float32)
    for group_index in range(N_HEADS):
        lower = group_index * group_width
        portion = jnp.dot(context_one[:, lower:lower + group_width], weight_one[lower:lower + group_width, :], preferred_element_type=jnp.float32)
        rounded = lax.optimization_barrier(portion.astype(jnp.bfloat16))
        running = running + rounded.astype(jnp.float32)
    return (running + skip_one.astype(jnp.float32)).astype(jnp.bfloat16)


def reference(context, out_weight, skip_states, gram_old, cross_old, map_old):
    source = model_states(context[0], out_weight[0], skip_states[0])
    target = model_states(context[1], out_weight[1], skip_states[1])
    new_weight = (1.0 - decay_keep) / TOKENS
    gram_new = decay_keep * gram_old + new_weight * jnp.dot(source.T, source, preferred_element_type=jnp.float32)
    cross_new = decay_keep * cross_old + new_weight * jnp.dot(source.T, target, preferred_element_type=jnp.float32)
    gram_half = gram_new.astype(jnp.bfloat16)
    map_half = map_old.astype(jnp.bfloat16)
    residual = cross_new - jnp.dot(gram_half, map_half, preferred_element_type=jnp.float32) - ridge_weight * map_old
    residual_half = residual.astype(jnp.bfloat16)
    applied = jnp.dot(gram_half, residual_half, preferred_element_type=jnp.float32) + ridge_weight * residual
    step_size = jnp.sum(residual * residual) / jnp.sum(residual * applied)
    map_new = map_old + step_size * residual
    residual_new = residual - step_size * applied
    return (gram_new, cross_new, map_new, residual_new)
```

```python
import jax
import jax.numpy as jnp
from jax import lax
from jax.sharding import PartitionSpec as P

decay_keep = 0.75
ridge_weight = 0.1
f32, bf16 = jnp.float32, jnp.bfloat16
CHUNKS = 4


def dot(a, b):
    return jnp.dot(a, b, preferred_element_type=f32)


def token_inner(left, right):
    return lax.dot_general(left, right, (((0,), (0,)), ((), ())), preferred_element_type=f32)


def shifted(block, axis, shift):
    n = lax.axis_size(axis)
    return lax.ppermute(block, axis, [(i, (i + shift) % n) for i in range(n)])


def total_over(value, axis):
    n = lax.axis_size(axis)
    if n & (n - 1):
        return lax.psum(value, axis)
    bit = 1
    while bit < n:
        value = value + lax.ppermute(value, axis, [(i, i ^ bit) for i in range(n)])
        bit *= 2
    return value


def sum_tok(value):
    n = lax.axis_size("tok")
    half = value.astype(bf16)
    for shift in range(1, n):
        value = value + shifted(half, "tok", shift).astype(f32)
    return value.astype(bf16)


def make_states(context, out_weight, skip_states, width):
    n_tok, n_heads, n_mp = (lax.axis_size(a) for a in ("tok", "heads", "mp"))
    t, h, k = (lax.axis_index(a) for a in ("tok", "heads", "mp"))
    tokens, features = skip_states.shape[1:]
    share = features // n_heads
    part = dot(context[0], out_weight[0]).astype(bf16)
    mine = lax.psum_scatter(part, "heads", scatter_dimension=1, tiled=True)
    skip = lax.dynamic_slice(skip_states, (k, 0, h * share), (1, tokens, share))[0]
    mine = (mine.astype(f32) + skip.astype(f32)).astype(bf16)
    other = lax.ppermute(mine, "mp", [(0, 1), (1, 0)])
    pair = jnp.stack([jnp.where(k == 0, mine, other), jnp.where(k == 0, other, mine)])
    if share == width and n_tok == n_mp == 2:
        away = lax.ppermute(pair, ("mp", "tok"), [(0, 1), (3, 2)])
        columns = jnp.where(k == t, pair, away)
        half = lax.dynamic_slice_in_dim(pair[0], k * (tokens // 2), tokens // 2, 0)
        rows = lax.all_gather(half, "heads", axis=1, tiled=True)
        rows_other = lax.ppermute(rows, "mp", [(0, 1), (1, 0)])
        first = jnp.where(k == 0, rows, rows_other)
        second = jnp.where(k == 0, rows_other, rows)
        source = jnp.concatenate([first, second], 0)
        return source, columns[0], columns[1]
    both = lax.all_gather(pair, "heads", axis=2, tiled=True)
    whole = lax.all_gather(both, "tok", axis=2, tiled=True)
    columns = lax.dynamic_slice_in_dim(whole, (k * n_heads + h) * width, width, 2)
    return both[0], columns[0], columns[1]


def per_device(context, out_weight, skip_states, gram_old, cross_old, map_old):
    n_tok = lax.axis_size("tok")
    t = lax.axis_index("tok")
    tokens = context.shape[1]
    height, width = gram_old.shape
    new_weight = (1.0 - decay_keep) / tokens
    step = height // CHUNKS
    cuts = [slice(c * step, (c + 1) * step) for c in range(CHUNKS)]

    map_half = map_old.astype(bf16)
    gram_old_half = gram_old.astype(bf16)
    panels = [lax.all_gather(gram_old_half[cut], ("mp", "heads"), axis=1, tiled=True) for cut in cuts]
    maps = [map_half] + [shifted(map_half, "tok", s) for s in range(1, n_tok)]
    source, source_cols, target_cols = make_states(context, out_weight, skip_states, width)

    gram_new = decay_keep * gram_old + new_weight * token_inner(source, source_cols)
    cross_new = decay_keep * cross_old + new_weight * token_inner(source, target_cols)

    def panel_part(panel, s):
        owner = lax.rem(t - s + n_tok, n_tok)
        return lax.dynamic_slice_in_dim(panel, owner * height, height, 1)

    inner_map = sum_tok(dot(source, map_half))
    residuals, halves = [], []
    for cut, panel in zip(cuts, panels):
        product = sum(dot(panel_part(panel, s), maps[s]) for s in range(n_tok))
        low_rank = token_inner(source[:, cut], inner_map)
        residual = (
            cross_new[cut] - decay_keep * product - new_weight * low_rank - ridge_weight * map_old[cut]
        )
        residuals.append(residual)
        halves.append(residual.astype(bf16))
    away = [[shifted(half, "tok", s) for half in halves] for s in range(1, n_tok)]
    inner_residual = sum_tok(sum(dot(source[:, cut], half) for cut, half in zip(cuts, halves)))
    blocks = [jnp.concatenate(halves, 0)] + [jnp.concatenate(a, 0) for a in away]
    applied, squares, mixed = [], 0.0, 0.0
    for cut, panel, residual in zip(cuts, panels, residuals):
        product = sum(dot(panel_part(panel, s), blocks[s]) for s in range(n_tok))
        low_rank = token_inner(source[:, cut], inner_residual)
        value = decay_keep * product + new_weight * low_rank + ridge_weight * residual
        applied.append(value)
        squares = squares + jnp.sum(residual * residual)
        mixed = mixed + jnp.sum(residual * value)
    totals = jnp.stack([squares, mixed])
    for axis in ("mp", "tok", "heads"):
        totals = total_over(totals, axis)
    step_size = totals[0] / totals[1]
    residual = jnp.concatenate(residuals, 0)
    return (
        gram_new,
        cross_new,
        map_old + step_size * residual,
        residual - step_size * jnp.concatenate(applied, 0),
    )


def solution(mesh):
    block = P("tok", ("mp", "heads"))
    placed = (P("mp", None, "heads"), P("mp", "heads", "tok"), P(None, None, "tok"), block, block, block)
    return jax.shard_map(
        per_device, mesh=mesh, in_specs=placed, out_specs=(block,) * 4, check_vma=False
    )
```

```python
import jax
import jax.numpy as jnp
from jax import lax
from jax.sharding import PartitionSpec as P

decay_keep = 0.75
ridge_weight = 0.1
f32, bf16 = jnp.float32, jnp.bfloat16
CHUNKS = 4


def dot(a, b):
    return jnp.dot(a, b, preferred_element_type=f32)


def token_inner(left, right):
    return lax.dot_general(left, right, (((0,), (0,)), ((), ())), preferred_element_type=f32)


def shifted(block, axis, shift):
    n = lax.axis_size(axis)
    return lax.ppermute(block, axis, [(i, (i + shift) % n) for i in range(n)])


def total_over(value, axis):
    n = lax.axis_size(axis)
    if n & (n - 1):
        return lax.psum(value, axis)
    bit = 1
    while bit < n:
        value = value + lax.ppermute(value, axis, [(i, i ^ bit) for i in range(n)])
        bit *= 2
    return value


def sum_tok(value):
    n = lax.axis_size("tok")
    half = value.astype(bf16)
    for shift in range(1, n):
        value = value + shifted(half, "tok", shift).astype(f32)
    return value.astype(bf16)


def scatter_sum(part, axis):
    n = lax.axis_size(axis)
    me = lax.axis_index(axis)
    share = part.shape[1] // n
    blocks = [part[:, i * share:(i + 1) * share] for i in range(n)]
    bit = 1
    while bit < n:
        mine = (me // bit) % 2 == 1
        keep = [jnp.where(mine, high, low) for low, high in zip(blocks[0::2], blocks[1::2])]
        send = [jnp.where(mine, low, high) for low, high in zip(blocks[0::2], blocks[1::2])]
        send = jnp.concatenate([block.astype(bf16) for block in send], 1)
        got = lax.ppermute(send, axis, [(i, i ^ bit) for i in range(n)]).astype(f32)
        blocks = [block.astype(f32) + got[:, i * share:(i + 1) * share] for i, block in enumerate(keep)]
        bit *= 2
    return blocks[0]


def gather_columns(block, axis):
    n = lax.axis_size(axis)
    me = lax.axis_index(axis)
    bit = n // 2
    blocks = [block]
    while bit:
        mine = (me // bit) % 2 == 1
        own = jnp.concatenate(blocks, 1)
        got = lax.ppermute(own, axis, [(i, i ^ bit) for i in range(n)])
        share = block.shape[1]
        got = [got[:, i * share:(i + 1) * share] for i in range(len(blocks))]
        low = [jnp.where(mine, g, o) for g, o in zip(got, blocks)]
        high = [jnp.where(mine, o, g) for g, o in zip(got, blocks)]
        blocks = [x for pair in zip(low, high) for x in pair]
        bit //= 2
    return jnp.concatenate(blocks, 1)


def make_states(context, out_weight, skip_states, width):
    n_tok, n_heads, n_mp = (lax.axis_size(a) for a in ("tok", "heads", "mp"))
    t, h, k = (lax.axis_index(a) for a in ("tok", "heads", "mp"))
    tokens, features = skip_states.shape[1:]
    share = features // n_heads
    part = dot(context[0], out_weight[0]).astype(bf16)
    mine = scatter_sum(part, "heads")
    skip = lax.dynamic_slice(skip_states, (k, 0, h * share), (1, tokens, share))[0]
    mine = (mine + skip.astype(f32)).astype(bf16)
    other = lax.ppermute(mine, "mp", [(0, 1), (1, 0)])
    pair = jnp.stack([jnp.where(k == 0, mine, other), jnp.where(k == 0, other, mine)])
    if share == width and n_tok == n_mp == 2:
        away = lax.ppermute(pair, ("mp", "tok"), [(0, 1), (3, 2)])
        columns = jnp.where(k == t, pair, away)
        half = lax.dynamic_slice_in_dim(pair[0], k * (tokens // 2), tokens // 2, 0)
        rows = gather_columns(half, "heads")
        rows_other = lax.ppermute(rows, "mp", [(0, 1), (1, 0)])
        first = jnp.where(k == 0, rows, rows_other)
        second = jnp.where(k == 0, rows_other, rows)
        source = jnp.concatenate([first, second], 0)
        return source, columns[0], columns[1]
    both = lax.all_gather(pair, "heads", axis=2, tiled=True)
    whole = lax.all_gather(both, "tok", axis=2, tiled=True)
    columns = lax.dynamic_slice_in_dim(whole, (k * n_heads + h) * width, width, 2)
    return both[0], columns[0], columns[1]


def per_device(context, out_weight, skip_states, gram_old, cross_old, map_old):
    n_tok = lax.axis_size("tok")
    t = lax.axis_index("tok")
    tokens = context.shape[1]
    height, width = gram_old.shape
    new_weight = (1.0 - decay_keep) / tokens
    step = height // CHUNKS
    cuts = [slice(c * step, (c + 1) * step) for c in range(CHUNKS)]

    map_half = map_old.astype(bf16)
    gram_old_half = gram_old.astype(bf16)
    gram_old_half, context = lax.optimization_barrier((gram_old_half, context))
    panel = lax.all_gather(gram_old_half, ("mp", "heads"), axis=1, tiled=True)
    maps = [map_half] + [shifted(map_half, "tok", s) for s in range(1, n_tok)]
    source, source_cols, target_cols = make_states(context, out_weight, skip_states, width)

    gram_new = decay_keep * gram_old + new_weight * token_inner(source, source_cols)
    cross_new = decay_keep * cross_old + new_weight * token_inner(source, target_cols)

    def panel_part(cut, s):
        owner = lax.rem(t - s + n_tok, n_tok)
        return lax.dynamic_slice(panel, (cut.start, owner * height), (step, height))

    inner_map = sum_tok(dot(source, map_half))
    residuals, halves = [], []
    for cut in cuts:
        product = sum(dot(panel_part(cut, s), maps[s]) for s in range(n_tok))
        low_rank = token_inner(source[:, cut], inner_map)
        residual = (
            cross_new[cut] - decay_keep * product - new_weight * low_rank - ridge_weight * map_old[cut]
        )
        residuals.append(residual)
        halves.append(residual.astype(bf16))
    away = [[shifted(half, "tok", s) for half in halves] for s in range(1, n_tok)]
    inner_residual = sum_tok(sum(dot(source[:, cut], half) for cut, half in zip(cuts, halves)))
    blocks = [jnp.concatenate(halves, 0)] + [jnp.concatenate(a, 0) for a in away]
    applied, squares, mixed = [], 0.0, 0.0
    for cut, residual in zip(cuts, residuals):
        product = sum(dot(panel_part(cut, s), blocks[s]) for s in range(n_tok))
        low_rank = token_inner(source[:, cut], inner_residual)
        value = decay_keep * product + new_weight * low_rank + ridge_weight * residual
        applied.append(value)
        squares = squares + jnp.sum(residual * residual)
        mixed = mixed + jnp.sum(residual * value)
    totals = jnp.stack([squares, mixed])
    for axis in ("mp", "tok", "heads"):
        totals = total_over(totals, axis)
    step_size = totals[0] / totals[1]
    residual = jnp.concatenate(residuals, 0)
    return (
        gram_new,
        cross_new,
        map_old + step_size * residual,
        residual - step_size * jnp.concatenate(applied, 0),
    )


def solution(mesh):
    block = P("tok", ("mp", "heads"))
    placed = (P("mp", None, "heads"), P("mp", "heads", "tok"), P(None, None, "tok"), block, block, block)
    return jax.shard_map(
        per_device, mesh=mesh, in_specs=placed, out_specs=(block,) * 4, check_vma=False
    )
```
